1024 devices in a mesh: cross: 16 (over z, y_lo), node: 64 (over y_hi, x, core).
Axes of the slice: x: 8, y: 8 (y_hi: 4, y_lo: 2; y = y_hi * 2 + y_lo), z: 8, core: 2. Of those that a mesh axis runs over, the one named last changes fastest.
Arguments:
- tokens: bfloat16 [131072, 12288], P(('cross', 'node')), may hold values from -24 to 24
- codes: bfloat16 [64, 12288], P(None, 'node'), may hold values from -0.0546875 to 0.0546875
- code_scale: float32 [1, 384], P(None, 'node'), may hold values from 0.25 to 4
- upstream: bfloat16 [131072, 64], P(('cross', 'node')), may hold values from -0.0390625 to 0.0390625
Outputs:
- values: bfloat16 [131072, 64], P(('cross', 'node'))
- weight_grad: float32 [12288, 64], P(('cross', 'node'))
The draws below stay inside these ranges and needn't reach their ends.
All inputs are finite; a program needn't handle non-finite values. Where the reference program divides by a largest or mean magnitude, that divisor is 1e-20 or more.
Results may differ from the reference program's by a relative error of at most 0.015.
Values may be sent and summed in bfloat16 or wider, within the bound.
No kernel may reach another device: no remote copies, remote signals or barrier semaphores. Data moves between devices by JAX's collectives and lax.ppermute only.
A program may use at most 64 MiB of HBM per device.

```python
import math
import jax
import jax.numpy as jnp
from jax import lax

D = 12288
HD = 64
TOK_DEV = 128
TOKENS = 131072
DEVICES = 1024


def strengthened(values, rng, source, target, blocks, factor):
    owner, partner = [(jnp.arange(values.shape[axis_at]) // (values.shape[axis_at] // blocks)).reshape([-1 if axis == axis_at else 1 for axis in range(values.ndim)]) for axis_at in (source, target)]
    chosen = jax.random.permutation(rng, blocks)[partner]
    strong = (owner == chosen) | (owner == (partner + blocks // 2) % blocks)
    return jnp.where(strong, factor * values, values)


def block_levels(own_key, extent, cuts, least, top_value):
    loudness, own = 1.0, jax.random.fold_in(own_key, 6)
    for axis_at, parts in cuts:
        steps = jnp.exp(jax.random.uniform(jax.random.fold_in(own, axis_at), (parts,), jnp.float32, least / len(cuts), top_value / len(cuts)))
        loudness = loudness * jnp.repeat(steps, extent[axis_at] // parts).reshape([-1 if axis == axis_at else 1 for axis in range(len(extent))])
    return loudness


def normal_values(rng, dims, scale, limit, split=(), dtype=jnp.bfloat16):
    entries = jax.random.normal(rng, dims, jnp.float32) * scale
    if len(split) > 0:
        entries = block_levels(rng, dims, split, -0.22, 0.18) * entries
    return jnp.clip(entries, min=-limit, max=limit).astype(dtype)


def gaussian_with(rng, extent, scale, most, cuts, heavy, kind=jnp.bfloat16):
    result = scale * jax.random.normal(rng, extent, jnp.float32)
    if cuts:
        result = result * block_levels(rng, extent, cuts, -0.22, 0.18)
    return jnp.clip(strengthened(result, jax.random.fold_in(rng, 3), *heavy), -most, most).astype(kind)


def setup_inputs(seed: int = 0) -> dict:
    key_list = jax.random.split(jax.random.key(seed), 5)
    return {
        "tokens": gaussian_with(key_list[0], (TOKENS, D), 1.0, 24.0, ((0, 1024),), (0, 1, 1024, 6.0)),
        "codes": normal_values(key_list[1], (HD, D), D ** -0.5, 0.0546875, ((1, 64),)),
        "code_scale": jnp.clip(jnp.exp(math.log(4.0) - 2.7725887 * jax.random.uniform(key_list[2], (1, D * HD // 2048), jnp.float32) ** block_levels(key_list[2], (1, D * HD // 2048), ((1, 64),), -0.2, 0.2)), 0.25, 4.0),
        "upstream": normal_values(key_list[3], (TOKENS, HD), (TOKENS ** -0.5), 0.0390625, ((0, 1024),)),
    }


def expand_weights(codes, code_scale):
    channels, width = codes.shape
    span = 2048 // channels
    blocks = codes.astype(jnp.float32).reshape(channels, width // span, span)
    scaled = blocks * code_scale.reshape(1, width // span, 1)
    return scaled.reshape(channels, width).astype(jnp.bfloat16)


def reference(tokens, codes, code_scale, upstream):
    weights = expand_weights(codes, code_scale)
    values = lax.dot_general(tokens, weights, (((1,), (1,)), ((), ())), preferred_element_type=jnp.float32).astype(jnp.bfloat16)
    span = 2048 // HD
    token_rows = tokens.reshape(DEVICES, TOK_DEV, D)
    upstream_rows = upstream.reshape(DEVICES, TOK_DEV, HD)

    def accumulate(total, pair):
        rows_x, rows_g = pair
        term = lax.dot_general(rows_x, rows_g, (((0,), (0,)), ((), ())), preferred_element_type=jnp.float32)
        blocks = term.reshape(D // span, span * HD)
        scale = jnp.max(jnp.abs(blocks), axis=1, keepdims=True) + 1e-6
        packed = (blocks / scale).astype(jnp.bfloat16)
        return total + (packed.astype(jnp.float32) * scale).reshape(D, HD), None

    weight_grad, unused = lax.scan(accumulate, jnp.zeros((D, HD), jnp.float32), (token_rows, upstream_rows))
    return values, weight_grad
```

```python
import jax
import jax.numpy as jnp
import numpy as np
from jax import lax
from jax.experimental import pallas as pl
from jax.experimental.pallas import tpu as pltpu
from jax.sharding import Mesh
from jax.sharding import PartitionSpec as P

AXES = ("z", "yl", "yh", "x", "c")
SIZES = (8, 2, 4, 8, 2)
D, HD, TOK = 12288, 64, 128
BF, F32 = jnp.bfloat16, jnp.float32
NT = (((1,), (1,)), ((), ()))
SPAN = 384


def groups():
    dev = np.arange(1024).reshape(8, 8, 8, 2)
    line = [dev[:, y, x, 0] for y in range(8) for x in range(8)] + [dev[z, :, x, 1] for z in range(8) for x in range(8)]
    plane = [dev[z, :, :, 0].reshape(-1) for z in range(8)] + [dev[:, y, :, 1].reshape(-1) for y in range(8)]
    return [g.tolist() for g in line], [g.tolist() for g in plane]


def scale_kernel(codes_ref, scale_ref, out_ref):
    lane = lax.broadcasted_iota(jnp.int32, (HD, 192), 1) // 32
    factor = jnp.full((HD, 192), scale_ref[0, 0], F32)
    for k in range(1, 6):
        factor = jnp.where(lane == k, scale_ref[0, k], factor)
    weights = (codes_ref[...].astype(F32) * factor).astype(BF)
    for k in range(8):
        out_ref[k] = weights


def pair_kernel(in_ref, out_ref):
    for k in range(4):
        out_ref[k, :, 0:192] = in_ref[2 * k]
        out_ref[k, :, 192:384] = in_ref[2 * k + 1]


def term_kernel(core_ref, tokens_ref, upstream_ref, out_ref):
    step = pl.program_id(0)
    core = core_ref[0]
    row = lax.broadcasted_iota(jnp.int32, (192, SPAN), 0)
    col = lax.broadcasted_iota(jnp.int32, (192, SPAN), 1)
    first = row + 12 * (row // 12)
    pick = jnp.concatenate([(col == first).astype(F32), (col == first + 12).astype(F32)], axis=1).astype(BF)
    blank = jnp.zeros((HD, SPAN), BF)
    for b in range(tokens_ref.shape[1] // SPAN):
        part = jnp.dot(upstream_ref[...], tokens_ref[:, SPAN * b : SPAN * (b + 1)], preferred_element_type=F32).astype(BF)
        both = jnp.concatenate(
            [jnp.concatenate([part, blank], axis=1), jnp.concatenate([blank, part], axis=1)], axis=0
        )
        rows = lax.dot_general(pick, both, NT, preferred_element_type=F32).astype(BF)
        for half in range(2):
            block = step * (tokens_ref.shape[1] // 192) + 2 * b + half
            z, y = block // 8, block % 8
            out_ref[jnp.where(core == 0, z * 8 + y, y * 8 + z)] = rows[96 * half : 96 * half + 96]


def sum_kernel(in_ref, out_ref, total_ref):
    total = in_ref[0].astype(F32)
    for k in range(1, 8):
        total += in_ref[k].astype(F32)
    total_ref[...] = total
    for k in range(out_ref.shape[0]):
        out_ref[k] = total_ref[12 * k : 12 * k + 12].astype(BF)


def values_kernel(weights_ref, tokens_ref, out_ref):
    total = jnp.zeros((HD, TOK), F32)
    for yh in range(4):
        for x in range(8):
            at = SPAN * (yh * 8 + x)
            total += lax.dot_general(
                weights_ref[x, yh], tokens_ref[:, at : at + SPAN], NT, preferred_element_type=F32
            )
    out_ref[...] = total.astype(BF)


def shards(tokens, codes, code_scale, upstream):
    line, plane = groups()
    core = lax.axis_index("c")
    vmem = pl.BlockSpec(memory_space=pltpu.VMEM)
    smem = pl.BlockSpec(memory_space=pltpu.SMEM)
    params = pltpu.CompilerParams(vmem_limit_bytes=40 * 2**20)

    copies = pl.pallas_call(
        scale_kernel,
        out_shape=jax.ShapeDtypeStruct((8, HD, 192), BF),
        in_specs=[vmem, smem],
        out_specs=vmem,
        name="scale",
    )(codes, code_scale)
    near = lax.all_to_all(copies, ("yh", "c"), split_axis=0, concat_axis=0, tiled=True)
    paired = pl.pallas_call(
        pair_kernel,
        out_shape=jax.ShapeDtypeStruct((4, HD, SPAN), BF),
        in_specs=[vmem],
        out_specs=vmem,
        name="pair",
    )(near)
    weights = lax.all_gather(paired, "x", axis=0, tiled=False)

    width = 3072
    term = pl.pallas_call(
        term_kernel,
        grid=(D // width,),
        out_shape=jax.ShapeDtypeStruct((64, 96, 128), BF),
        in_specs=[
            smem,
            pl.BlockSpec((TOK, width), lambda i: (0, i)),
            pl.BlockSpec((HD, TOK), lambda i: (0, 0)),
        ],
        out_specs=pl.BlockSpec((64, 96, 128), lambda i: (0, 0, 0)),
        compiler_params=params,
        cost_estimate=pl.CostEstimate(flops=2 * D * TOK * HD, bytes_accessed=5 * 2**20, transcendentals=0),
        name="term",
    )(core.reshape(1), tokens, upstream.T)
    arrived = lax.all_to_all(
        term.reshape(8, 768, 128), AXES, split_axis=0, concat_axis=0, axis_index_groups=line, tiled=True
    )
    partial_sum = pl.pallas_call(
        sum_kernel,
        grid=(4,),
        out_shape=jax.ShapeDtypeStruct((64, 12, 128), BF),
        in_specs=[pl.BlockSpec((8, 192, 128), lambda i: (0, i, 0))],
        out_specs=pl.BlockSpec((16, 12, 128), lambda i: (i, 0, 0)),
        scratch_shapes=[pltpu.VMEM((192, 128), F32)],
        compiler_params=params,
        cost_estimate=pl.CostEstimate(flops=2 * D * HD, bytes_accessed=2 * 2**20, transcendentals=0),
        name="sum",
    )(arrived)
    last = lax.all_to_all(partial_sum, AXES, split_axis=0, concat_axis=0, axis_index_groups=plane, tiled=True)
    chip = lax.psum(jnp.sum(last.astype(F32), axis=0), "c")
    weight_grad = jnp.where(core == 0, chip[:, :HD], chip[:, HD:])

    values = pl.pallas_call(
        values_kernel,
        out_shape=jax.ShapeDtypeStruct((HD, TOK), BF),
        in_specs=[vmem, vmem],
        out_specs=vmem,
        compiler_params=params,
        cost_estimate=pl.CostEstimate(flops=2 * D * TOK * HD, bytes_accessed=5 * 2**20, transcendentals=0),
        name="values",
    )(weights, tokens)
    return values.T, weight_grad


def solution(mesh):
    fine = Mesh(mesh.devices.reshape(SIZES), AXES)
    rows = P(AXES, None)
    columns = P(None, ("yh", "x", "c"))
    return jax.shard_map(
        shards, mesh=fine, in_specs=(rows, columns, columns, rows), out_specs=(rows, rows), check_vma=False
    )
```

```python
import jax
import jax.numpy as jnp
import numpy as np
from jax import lax
from jax.experimental import pallas as pl
from jax.experimental.pallas import tpu as pltpu
from jax.sharding import Mesh
from jax.sharding import PartitionSpec as P

AXES = ("z", "yl", "yh", "x", "c")
SIZES = (8, 2, 4, 8, 2)
D, HD, TOK = 12288, 64, 128
BF, F32 = jnp.bfloat16, jnp.float32
NT = (((1,), (1,)), ((), ()))
SPAN = 384


def groups():
    dev = np.arange(1024).reshape(SIZES)
    whole = dev.transpose(0, 2, 1, 3, 4).reshape(8, 8, 8, 2)
    near = [
        np.array([[dev[pz + 2 * (t ^ (yh // 2 * 2 + x // 2)), yl, yh, 2 * x + px, c] for x in range(4)] for yh in range(4)]).reshape(-1)
        for t in range(4)
        for pz, yl, px, c in np.ndindex(2, 2, 2, 2)
    ]
    rest = [dev[pz::2, yl, :, px::2, c].reshape(-1) for c in range(2) for pz in range(2) for yl in range(2) for px in range(2)]
    cube = []
    for core in range(2):
        for base in np.ndindex(4, 4, 4):
            corner = [2 * i + core for i in base]
            members = {}
            for step in np.ndindex(2, 2, 2):
                z, y, x = [(i + j) % 8 for i, j in zip(corner, step)]
                members[z % 2 * 4 + y % 2 * 2 + x % 2] = whole[z, y, x, core]
            cube.append(np.array([members[k] for k in range(8)]))
    return [[g.tolist() for g in kind] for kind in (near, cube, rest)]


def scale_kernel(at_ref, codes_ref, scale_ref, out_ref):
    lane = lax.broadcasted_iota(jnp.int32, (16, 192), 1) // 32
    factor = jnp.full((16, 192), scale_ref[0, 0], F32)
    for k in range(1, 6):
        factor = jnp.where(lane == k, scale_ref[0, k], factor)
    rows = codes_ref[pl.ds(pl.multiple_of(at_ref[0], 16), 16), :]
    weights = (rows.astype(F32) * factor).astype(BF)
    for k in range(16):
        out_ref[k] = weights


def term_kernel(core_ref, tokens_hbm, upstream_ref, own_hbm, send_hbm, tokens_ref, part_ref, out_ref, in_sem, out_sem):
    core = core_ref[0]
    reads = [
        pltpu.make_async_copy(tokens_hbm.at[:, 1536 * z : 1536 * (z + 1)], tokens_ref.at[z], in_sem.at[z])
        for z in range(8)
    ]
    for read in reads:
        read.start()
    source = lax.broadcasted_iota(jnp.int32, (768, 768), 0)
    place = lax.broadcasted_iota(jnp.int32, (768, 768), 1)
    line = source // 12
    target = 12 * (32 * (line % 2) + 16 * (line // 2 % 2) + line // 4) + source % 12
    move = (place == target).astype(F32).astype(BF)
    writes = []
    for half in range(2):
        for z in range(4):
            reads[4 * half + z].wait()
            part = jnp.dot(upstream_ref[...], tokens_ref[4 * half + z], preferred_element_type=F32).astype(BF)
            for yl in range(2):
                part_ref[HD * (2 * z + yl) : HD * (2 * z + yl + 1)] = part[:, 768 * yl : 768 * (yl + 1)]
        for owner in range(2):
            moved = jnp.dot(
                part_ref[...], move[:, SPAN * owner : SPAN * (owner + 1)], preferred_element_type=F32
            ).astype(BF)
            for z in range(4):
                for yl in range(2):
                    for px in range(2):
                        k = z % 2 * 4 + yl * 2 + px
                        at = SPAN * half + 192 * (z // 2)
                        out_ref[owner, k, :, at : at + 192] = moved[
                            HD * (2 * z + yl) : HD * (2 * z + yl + 1), 192 * px : 192 * (px + 1)
                        ]
        at = pl.ds(SPAN * half, SPAN)
        for i, (owner, out_hbm) in enumerate(((1 - core, send_hbm), (core, own_hbm))):
            writes.append(
                pltpu.make_async_copy(out_ref.at[owner, :, :, at], out_hbm.at[:, :, at], out_sem.at[2 * half + i])
            )
            writes[-1].start()
    for write in writes:
        write.wait()


def fill_kernel(near_ref, own_ref, other_ref, out_ref):
    out_ref[:, :, :768] = (own_ref[...].astype(F32) + other_ref[...].astype(F32)).astype(BF)
    for p in range(out_ref.shape[0]):
        for k in range(16):
            out_ref[p, 16 * (k // 4) : 16 * (k // 4 + 1), 768 + 192 * (k % 4) : 960 + 192 * (k % 4)] = near_ref[k]


def sum_kernel(in_ref, in_hbm, out_ref, weights_hbm, sem):
    step = pl.program_id(0)
    copy = pltpu.make_async_copy(in_hbm.at[:, :, pl.ds(768, 768)], weights_hbm, sem)

    @pl.when(step == 0)
    def _():
        copy.start()

    row = lax.broadcasted_iota(jnp.int32, (256, SPAN), 0)
    col = lax.broadcasted_iota(jnp.int32, (256, SPAN), 1)
    first = jnp.where(row % 8 < 6, 12 * (row // 8) + row % 8, -SPAN)
    pick = jnp.concatenate([(col == first).astype(F32), (col == first + 6).astype(F32)], axis=1).astype(BF)
    total = in_ref[0].astype(F32)
    for k in range(1, 8):
        total += in_ref[k].astype(F32)
    total = total.astype(BF)
    blank = jnp.zeros((HD, SPAN), BF)
    both = jnp.concatenate(
        [jnp.concatenate([total, blank], axis=1), jnp.concatenate([blank, total], axis=1)], axis=0
    )
    rows = lax.dot_general(pick, both, NT, preferred_element_type=F32)
    out_ref[...] = rows.reshape(32, 8, 128).astype(BF)

    @pl.when(step == 1)
    def _():
        copy.wait()


def values_kernel(core_ref, own_ref, other_ref, tokens_ref, out_ref):
    def product(first_ref, second_ref):
        total = jnp.zeros((HD, TOK), F32)
        for yh in range(4):
            for x in range(8):
                at = SPAN * (yh * 8 + x)
                halves = [
                    jnp.concatenate(
                        [
                            ref[2 * q + x % 2, 16 * yh : 16 * (yh + 1), 192 * (x // 2) : 192 * (x // 2 + 1)]
                            for q in range(4)
                        ],
                        axis=0,
                    )
                    for ref in (first_ref, second_ref)
                ]
                total += lax.dot_general(
                    jnp.concatenate(halves, axis=1), tokens_ref[:, at : at + SPAN], NT, preferred_element_type=F32
                )
        out_ref[...] = total.astype(BF)

    @pl.when(core_ref[0] == 0)
    def _():
        product(own_ref, other_ref)

    @pl.when(core_ref[0] != 0)
    def _():
        product(other_ref, own_ref)


def final_kernel(in_ref, out_ref):
    total = in_ref[0].astype(F32)
    for k in range(1, 64):
        total += in_ref[k].astype(F32)
    out_ref[0:6] = total[0:6, :HD]
    out_ref[6:12] = total[0:6, HD:]


def shards(tokens, codes, code_scale, upstream):
    near_groups, cube, rest = groups()
    core = lax.axis_index("c").reshape(1)
    vmem = pl.BlockSpec(memory_space=pltpu.VMEM)
    smem = pl.BlockSpec(memory_space=pltpu.SMEM)
    hbm = pl.BlockSpec(memory_space=pl.ANY)

    def exchange(value, who):
        return lax.all_to_all(value, AXES, split_axis=0, concat_axis=0, axis_index_groups=who, tiled=True)

    def swap(value):
        return lax.ppermute(value, "c", [(0, 1), (1, 0)])

    at = 16 * (2 * (lax.axis_index("z") % 2) + lax.axis_index("yl"))
    near = exchange(
        pl.pallas_call(
            scale_kernel,
            out_shape=jax.ShapeDtypeStruct((16, 16, 192), BF),
            in_specs=[smem, vmem, smem],
            out_specs=vmem,
            name="scale",
        )(at.reshape(1), codes, code_scale),
        near_groups,
    )
    own, send = pl.pallas_call(
        term_kernel,
        out_shape=[jax.ShapeDtypeStruct((8, HD, 768), BF)] * 2,
        in_specs=[smem, hbm, vmem],
        out_specs=[hbm, hbm],
        scratch_shapes=[
            pltpu.VMEM((8, TOK, 1536), BF),
            pltpu.VMEM((8 * HD, 768), BF),
            pltpu.VMEM((2, 8, HD, 768), BF),
            pltpu.SemaphoreType.DMA((8,)),
            pltpu.SemaphoreType.DMA((4,)),
        ],
        compiler_params=pltpu.CompilerParams(vmem_limit_bytes=60 * 2**20),
        cost_estimate=pl.CostEstimate(flops=2 * D * TOK * HD, bytes_accessed=5 * 2**20, transcendentals=0),
        name="term",
    )(core, tokens, upstream.T)
    send, near = lax.optimization_barrier((send, near))
    part = pl.BlockSpec((4, HD, 768), lambda i: (i, 0, 0))
    outgoing = pl.pallas_call(
        fill_kernel,
        grid=(2,),
        out_shape=jax.ShapeDtypeStruct((8, HD, 1536), BF),
        in_specs=[pl.BlockSpec((16, 16, 192), lambda i: (0, 0, 0)), part, part],
        out_specs=pl.BlockSpec((4, HD, 1536), lambda i: (i, 0, 0)),
        compiler_params=pltpu.CompilerParams(vmem_limit_bytes=40 * 2**20),
        name="fill",
    )(near, own, swap(send))
    arrived = exchange(outgoing, cube)
    partial_sum, weights = pl.pallas_call(
        sum_kernel,
        grid=(2,),
        out_shape=(jax.ShapeDtypeStruct((64, 8, 128), BF), jax.ShapeDtypeStruct((8, HD, 768), BF)),
        in_specs=[pl.BlockSpec((8, HD, SPAN), lambda i: (0, 0, i)), hbm],
        out_specs=(pl.BlockSpec((32, 8, 128), lambda i: (i, 0, 0)), hbm),
        scratch_shapes=[pltpu.SemaphoreType.DMA],
        compiler_params=pltpu.CompilerParams(vmem_limit_bytes=40 * 2**20),
        cost_estimate=pl.CostEstimate(flops=2 * D * HD, bytes_accessed=2 * 2**20, transcendentals=0),
        name="sum",
    )(arrived, arrived)
    last = exchange(partial_sum, rest)
    values = pl.pallas_call(
        values_kernel,
        out_shape=jax.ShapeDtypeStruct((HD, TOK), BF),
        in_specs=[smem, vmem, vmem, vmem],
        out_specs=vmem,
        compiler_params=pltpu.CompilerParams(vmem_limit_bytes=40 * 2**20),
        cost_estimate=pl.CostEstimate(flops=2 * D * TOK * HD, bytes_accessed=5 * 2**20, transcendentals=0),
        name="values",
    )(core, weights, swap(weights), tokens)
    last, values = lax.optimization_barrier((last, values))
    weight_grad = pl.pallas_call(
        final_kernel,
        out_shape=jax.ShapeDtypeStruct((12, HD), F32),
        in_specs=[vmem],
        out_specs=vmem,
        compiler_params=pltpu.CompilerParams(vmem_limit_bytes=4 * 2**20),
        name="final",
    )(last)
    return values.T, weight_grad


def solution(mesh):
    fine = Mesh(mesh.devices.reshape(SIZES), AXES)
    rows = P(AXES, None)
    columns = P(None, ("yh", "x", "c"))
    return jax.shard_map(
        shards, mesh=fine, in_specs=(rows, columns, columns, rows), out_specs=(rows, rows), check_vma=False
    )
```

```python
import jax
import jax.numpy as jnp
import numpy as np
from jax import lax
from jax.experimental import pallas as pl
from jax.experimental.pallas import tpu as pltpu
from jax.sharding import Mesh
from jax.sharding import PartitionSpec as P

AXES = ("z", "yl", "yh", "x", "c")
SIZES = (8, 2, 4, 8, 2)
D, HD, TOK = 12288, 64, 128
BF, F32 = jnp.bfloat16, jnp.float32
NT = (((1,), (1,)), ((), ()))
SPAN = 384


def groups():
    dev = np.arange(1024).reshape(SIZES)
    whole = dev.transpose(0, 2, 1, 3, 4).reshape(8, 8, 8, 2)
    near = [dev[z, yl, :, px::2, c].reshape(-1) for c in range(2) for z in range(8) for yl in range(2) for px in range(2)]
    rest = [dev[pz::2, yl, :, px::2, c].reshape(-1) for c in range(2) for pz in range(2) for yl in range(2) for px in range(2)]
    cube = []
    for core in range(2):
        for base in np.ndindex(4, 4, 4):
            corner = [2 * i + core for i in base]
            members = {}
            for step in np.ndindex(2, 2, 2):
                z, y, x = [(i + j) % 8 for i, j in zip(corner, step)]
                members[z % 2 * 4 + y % 2 * 2 + x % 2] = whole[z, y, x, core]
            cube.append(np.array([members[k] for k in range(8)]))
    return [[g.tolist() for g in kind] for kind in (near, cube, rest)]


def scale_kernel(at_ref, codes_ref, scale_ref, out_ref):
    lane = lax.broadcasted_iota(jnp.int32, (16, 192), 1) // 32
    factor = jnp.full((16, 192), scale_ref[0, 0], F32)
    for k in range(1, 6):
        factor = jnp.where(lane == k, scale_ref[0, k], factor)
    rows = codes_ref[pl.ds(pl.multiple_of(at_ref[0], 16), 16), :]
    weights = (rows.astype(F32) * factor).astype(BF)
    for k in range(16):
        out_ref[k] = weights


def term_kernel(core_ref, tokens_hbm, upstream_ref, own_hbm, send_hbm, tokens_ref, part_ref, out_ref, in_sem, out_sem):
    core = core_ref[0]
    reads = [
        pltpu.make_async_copy(tokens_hbm.at[:, 1536 * z : 1536 * (z + 1)], tokens_ref.at[z], in_sem.at[z])
        for z in range(8)
    ]
    for read in reads:
        read.start()
    source = lax.broadcasted_iota(jnp.int32, (768, 1), 0)
    place = lax.broadcasted_iota(jnp.int32, (768, 768), 1)
    line = source // 12
    target = 12 * (32 * (line % 2) + 16 * (line // 2 % 2) + line // 4) + source % 12
    move = (place == target).astype(F32).astype(BF)
    writes = []
    for half in range(2):
        for z in range(4):
            reads[4 * half + z].wait()
            part = jnp.dot(upstream_ref[...], tokens_ref[4 * half + z], preferred_element_type=F32).astype(BF)
            for yl in range(2):
                part_ref[HD * (2 * z + yl) : HD * (2 * z + yl + 1)] = part[:, 768 * yl : 768 * (yl + 1)]
        for owner in range(2):
            moved = jnp.dot(
                part_ref[...], move[:, SPAN * owner : SPAN * (owner + 1)], preferred_element_type=F32
            ).astype(BF)
            for z in range(4):
                for yl in range(2):
                    for px in range(2):
                        k = z % 2 * 4 + yl * 2 + px
                        at = SPAN * half + 192 * (z // 2)
                        out_ref[owner, k, :, at : at + 192] = moved[
                            HD * (2 * z + yl) : HD * (2 * z + yl + 1), 192 * px : 192 * (px + 1)
                        ]
        at = pl.ds(SPAN * half, SPAN)
        for i, (owner, out_hbm) in enumerate(((1 - core, send_hbm), (core, own_hbm))):
            writes.append(
                pltpu.make_async_copy(out_ref.at[owner, :, :, at], out_hbm.at[:, :, at], out_sem.at[2 * half + i])
            )
            writes[-1].start()
    for write in writes:
        write.wait()


def fill_kernel(near_ref, own_ref, other_ref, out_ref):
    out_ref[:, :, :768] = (own_ref[...].astype(F32) + other_ref[...].astype(F32)).astype(BF)
    for p in range(out_ref.shape[0]):
        for k in range(16):
            out_ref[p, 16 * (k // 4) : 16 * (k // 4 + 1), 768 + 192 * (k % 4) : 960 + 192 * (k % 4)] = near_ref[k]


def sum_kernel(in_ref, in_hbm, out_ref, weights_hbm, sem):
    step = pl.program_id(0)
    copy = pltpu.make_async_copy(in_hbm.at[:, :, pl.ds(768, 768)], weights_hbm, sem)

    @pl.when(step == 0)
    def _():
        copy.start()

    row = lax.broadcasted_iota(jnp.int32, (256, 1), 0)
    col = lax.broadcasted_iota(jnp.int32, (256, SPAN), 1)
    first = jnp.where(row % 8 < 6, 12 * (row // 8) + row % 8, -SPAN)
    pick = jnp.concatenate([(col == first).astype(F32), (col == first + 6).astype(F32)], axis=1).astype(BF)
    total = in_ref[0].astype(F32)
    for k in range(1, 8):
        total += in_ref[k].astype(F32)
    total = total.astype(BF)
    blank = jnp.zeros((HD, SPAN), BF)
    both = jnp.concatenate(
        [jnp.concatenate([total, blank], axis=1), jnp.concatenate([blank, total], axis=1)], axis=0
    )
    rows = lax.dot_general(pick, both, NT, preferred_element_type=F32)
    out_ref[...] = rows.reshape(32, 8, 128).astype(BF)

    @pl.when(step == 1)
    def _():
        copy.wait()


def values_kernel(core_ref, own_ref, other_ref, tokens_ref, out_ref):
    def product(first_ref, second_ref):
        total = jnp.zeros((HD, TOK), F32)
        for yh in range(4):
            for x in range(8):
                at = SPAN * (yh * 8 + x)
                halves = [
                    jnp.concatenate(
                        [
                            ref[2 * q + x % 2, 16 * yh : 16 * (yh + 1), 192 * (x // 2) : 192 * (x // 2 + 1)]
                            for q in range(4)
                        ],
                        axis=0,
                    )
                    for ref in (first_ref, second_ref)
                ]
                total += lax.dot_general(
                    jnp.concatenate(halves, axis=1), tokens_ref[:, at : at + SPAN], NT, preferred_element_type=F32
                )
        out_ref[...] = total.astype(BF)

    @pl.when(core_ref[0] == 0)
    def _():
        product(own_ref, other_ref)

    @pl.when(core_ref[0] != 0)
    def _():
        product(other_ref, own_ref)


def final_kernel(in_ref, out_ref):
    total = in_ref[0].astype(F32)
    for k in range(1, 64):
        total += in_ref[k].astype(F32)
    out_ref[0:6] = total[0:6, :HD]
    out_ref[6:12] = total[0:6, HD:]


def shards(tokens, codes, code_scale, upstream):
    near_groups, cube, rest = groups()
    core = lax.axis_index("c").reshape(1)
    vmem = pl.BlockSpec(memory_space=pltpu.VMEM)
    smem = pl.BlockSpec(memory_space=pltpu.SMEM)
    hbm = pl.BlockSpec(memory_space=pl.ANY)

    def exchange(value, who):
        return lax.all_to_all(value, AXES, split_axis=0, concat_axis=0, axis_index_groups=who, tiled=True)

    def swap(value):
        return lax.ppermute(value, "c", [(0, 1), (1, 0)])

    at = 16 * (2 * (lax.axis_index("z") % 2) + lax.axis_index("yl"))
    near = exchange(
        pl.pallas_call(
            scale_kernel,
            out_shape=jax.ShapeDtypeStruct((16, 16, 192), BF),
            in_specs=[smem, vmem, smem],
            out_specs=vmem,
            name="scale",
        )(at.reshape(1), codes, code_scale),
        near_groups,
    )
    own, send = pl.pallas_call(
        term_kernel,
        out_shape=[jax.ShapeDtypeStruct((8, HD, 768), BF)] * 2,
        in_specs=[smem, hbm, vmem],
        out_specs=[hbm, hbm],
        scratch_shapes=[
            pltpu.VMEM((8, TOK, 1536), BF),
            pltpu.VMEM((8 * HD, 768), BF),
            pltpu.VMEM((2, 8, HD, 768), BF),
            pltpu.SemaphoreType.DMA((8,)),
            pltpu.SemaphoreType.DMA((4,)),
        ],
        compiler_params=pltpu.CompilerParams(vmem_limit_bytes=60 * 2**20),
        cost_estimate=pl.CostEstimate(flops=2 * D * TOK * HD, bytes_accessed=5 * 2**20, transcendentals=0),
        name="term",
    )(core, tokens, upstream.T)
    send, near = lax.optimization_barrier((send, near))
    part = pl.BlockSpec((4, HD, 768), lambda i: (i, 0, 0))
    outgoing = pl.pallas_call(
        fill_kernel,
        grid=(2,),
        out_shape=jax.ShapeDtypeStruct((8, HD, 1536), BF),
        in_specs=[pl.BlockSpec((16, 16, 192), lambda i: (0, 0, 0)), part, part],
        out_specs=pl.BlockSpec((4, HD, 1536), lambda i: (i, 0, 0)),
        compiler_params=pltpu.CompilerParams(vmem_limit_bytes=40 * 2**20),
        name="fill",
    )(near, own, swap(send))
    arrived = exchange(outgoing, cube)
    partial_sum, weights = pl.pallas_call(
        sum_kernel,
        grid=(2,),
        out_shape=(jax.ShapeDtypeStruct((64, 8, 128), BF), jax.ShapeDtypeStruct((8, HD, 768), BF)),
        in_specs=[pl.BlockSpec((8, HD, SPAN), lambda i: (0, 0, i)), hbm],
        out_specs=(pl.BlockSpec((32, 8, 128), lambda i: (i, 0, 0)), hbm),
        scratch_shapes=[pltpu.SemaphoreType.DMA],
        compiler_params=pltpu.CompilerParams(vmem_limit_bytes=40 * 2**20),
        cost_estimate=pl.CostEstimate(flops=2 * D * HD, bytes_accessed=2 * 2**20, transcendentals=0),
        name="sum",
    )(arrived, arrived)
    last = exchange(partial_sum, rest)
    values = pl.pallas_call(
        values_kernel,
        out_shape=jax.ShapeDtypeStruct((HD, TOK), BF),
        in_specs=[smem, vmem, vmem, vmem],
        out_specs=vmem,
        compiler_params=pltpu.CompilerParams(vmem_limit_bytes=40 * 2**20),
        cost_estimate=pl.CostEstimate(flops=2 * D * TOK * HD, bytes_accessed=5 * 2**20, transcendentals=0),
        name="values",
    )(core, weights, swap(weights), tokens)
    last, values = lax.optimization_barrier((last, values))
    weight_grad = pl.pallas_call(
        final_kernel,
        out_shape=jax.ShapeDtypeStruct((12, HD), F32),
        in_specs=[vmem],
        out_specs=vmem,
        compiler_params=pltpu.CompilerParams(vmem_limit_bytes=4 * 2**20),
        name="final",
    )(last)
    return values.T, weight_grad


def solution(mesh):
    fine = Mesh(mesh.devices.reshape(SIZES), AXES)
    rows = P(AXES, None)
    columns = P(None, ("yh", "x", "c"))
    return jax.shard_map(
        shards, mesh=fine, in_specs=(rows, columns, columns, rows), out_specs=(rows, rows), check_vma=False
    )
```

```python
import jax
import jax.numpy as jnp
import numpy as np
from jax import lax
from jax.experimental import pallas as pl
from jax.experimental.pallas import tpu as pltpu
from jax.sharding import Mesh
from jax.sharding import PartitionSpec as P

AXES = ("z", "yl", "yh", "x", "c")
SIZES = (8, 2, 4, 8, 2)
D, HD, TOK = 12288, 64, 128
SHARE = 2
BF, F32 = jnp.bfloat16, jnp.float32
NT = (((1,), (1,)), ((), ()))
SPAN = 384


def groups():
    dev = np.arange(1024).reshape(SIZES)
    whole = dev.transpose(0, 2, 1, 3, 4).reshape(8, 8, 8, 2)
    near = [dev[z, yl, :, px::2, c].reshape(-1) for c in range(2) for z in range(8) for yl in range(2) for px in range(2)]
    rest = [dev[pz::2, yl, :, px::2, c].reshape(-1) for c in range(2) for pz in range(2) for yl in range(2) for px in range(2)]
    cube = []
    for core in range(2):
        for base in np.ndindex(4, 4, 4):
            corner = [2 * i + core for i in base]
            members = {}
            for step in np.ndindex(2, 2, 2):
                z, y, x = [(i + j) % 8 for i, j in zip(corner, step)]
                members[z % 2 * 4 + y % 2 * 2 + x % 2] = whole[z, y, x, core]
            cube.append(np.array([members[k] for k in range(8)]))
    return [[g.tolist() for g in kind] for kind in (near, cube, rest)]


def scale_kernel(at_ref, codes_ref, scale_ref, out_ref):
    lane = lax.broadcasted_iota(jnp.int32, (16, 192), 1) // 32
    factor = jnp.full((16, 192), scale_ref[0, 0], F32)
    for k in range(1, 6):
        factor = jnp.where(lane == k, scale_ref[0, k], factor)
    rows = codes_ref[pl.ds(pl.multiple_of(at_ref[0], 16), 16), :]
    weights = (rows.astype(F32) * factor).astype(BF)
    for k in range(16):
        out_ref[k] = weights


def term_kernel(core_ref, tokens_hbm, upstream_ref, own_hbm, send_hbm, tokens_ref, part_ref, out_ref, in_sem, out_sem):
    core = core_ref[0]
    reads = [
        pltpu.make_async_copy(tokens_hbm.at[:, 1536 * z : 1536 * (z + 1)], tokens_ref.at[z], in_sem.at[z])
        for z in range(8)
    ]
    for read in reads:
        read.start()
    source = lax.broadcasted_iota(jnp.int32, (768, 1), 0)
    place = lax.broadcasted_iota(jnp.int32, (768, 768), 1)
    line = source // 12
    target = 12 * (32 * (line % 2) + 16 * (line // 2 % 2) + line // 4) + source % 12
    move = (place == target).astype(F32).astype(BF)
    writes = []
    for half in range(2):
        for z in range(4):
            reads[4 * half + z].wait()
            part = jnp.dot(upstream_ref[...], tokens_ref[4 * half + z], preferred_element_type=F32).astype(BF)
            for yl in range(2):
                part_ref[HD * (2 * z + yl) : HD * (2 * z + yl + 1)] = part[:, 768 * yl : 768 * (yl + 1)]
        for owner in range(2):
            moved = jnp.dot(
                part_ref[...], move[:, SPAN * owner : SPAN * (owner + 1)], preferred_element_type=F32
            ).astype(BF)
            for z in range(4):
                for yl in range(2):
                    for px in range(2):
                        k = z % 2 * 4 + yl * 2 + px
                        at = SPAN * half + 192 * (z // 2)
                        out_ref[owner, k, :, at : at + 192] = moved[
                            HD * (2 * z + yl) : HD * (2 * z + yl + 1), 192 * px : 192 * (px + 1)
                        ]
        at = pl.ds(SPAN * half, SPAN)
        for i, (owner, out_hbm) in enumerate(((1 - core, send_hbm), (core, own_hbm))):
            writes.append(
                pltpu.make_async_copy(out_ref.at[owner, :, :, at], out_hbm.at[:, :, at], out_sem.at[2 * half + i])
            )
            writes[-1].start()
    for write in writes:
        write.wait()


def fill_kernel(near_ref, own_ref, other_ref, out_ref):
    out_ref[:, :, :768] = (own_ref[...].astype(F32) + other_ref[...].astype(F32)).astype(BF)
    for p in range(out_ref.shape[0]):
        for k in range(16):
            out_ref[p, 16 * (k // 4) : 16 * (k // 4 + 1), 768 + 192 * (k % 4) : 960 + 192 * (k % 4)] = near_ref[k]


def sum_kernel(in_ref, in_hbm, out_ref, *refs):
    step = pl.program_id(0)
    weights, sem = refs[:-1], refs[-1]
    copies = [
        pltpu.make_async_copy(in_hbm.at[pl.ds(SHARE * i, SHARE), :, pl.ds(768, 768)], piece, sem.at[i])
        for i, piece in enumerate(weights)
    ]

    @pl.when(step == 0)
    def _():
        for copy in copies:
            copy.start()

    row = lax.broadcasted_iota(jnp.int32, (256, 1), 0)
    col = lax.broadcasted_iota(jnp.int32, (256, SPAN), 1)
    first = jnp.where(row % 8 < 6, 12 * (row // 8) + row % 8, -SPAN)
    pick = jnp.concatenate([(col == first).astype(F32), (col == first + 6).astype(F32)], axis=1).astype(BF)
    total = in_ref[0].astype(F32)
    for k in range(1, 8):
        total += in_ref[k].astype(F32)
    total = total.astype(BF)
    blank = jnp.zeros((HD, SPAN), BF)
    both = jnp.concatenate(
        [jnp.concatenate([total, blank], axis=1), jnp.concatenate([blank, total], axis=1)], axis=0
    )
    rows = lax.dot_general(pick, both, NT, preferred_element_type=F32)
    out_ref[...] = rows.reshape(32, 8, 128).astype(BF)

    @pl.when(step == 1)
    def _():
        for copy in copies:
            copy.wait()


def values_kernel(core_ref, *refs):
    tokens_ref, out_ref = refs[-2:]
    own, other = refs[: 8 // SHARE], refs[8 // SHARE : -2]

    def product(first, second):
        total = jnp.zeros((HD, TOK), F32)
        for yh in range(4):
            for x in range(8):
                at = SPAN * (yh * 8 + x)
                halves = [
                    jnp.concatenate(
                        [
                            pieces[(2 * q + x % 2) // SHARE][(2 * q + x % 2) % SHARE, 16 * yh : 16 * (yh + 1), 192 * (x // 2) : 192 * (x // 2 + 1)]
                            for q in range(4)
                        ],
                        axis=0,
                    )
                    for pieces in (first, second)
                ]
                total += lax.dot_general(
                    jnp.concatenate(halves, axis=1), tokens_ref[:, at : at + SPAN], NT, preferred_element_type=F32
                )
        out_ref[...] = total.astype(BF)

    @pl.when(core_ref[0] == 0)
    def _():
        product(own, other)

    @pl.when(core_ref[0] != 0)
    def _():
        product(other, own)


def final_kernel(in_ref, out_ref):
    total = in_ref[0].astype(F32)
    for k in range(1, 64):
        total += in_ref[k].astype(F32)
    out_ref[0:6] = total[0:6, :HD]
    out_ref[6:12] = total[0:6, HD:]


def shards(tokens, codes, code_scale, upstream):
    near_groups, cube, rest = groups()
    core = lax.axis_index("c").reshape(1)
    vmem = pl.BlockSpec(memory_space=pltpu.VMEM)
    smem = pl.BlockSpec(memory_space=pltpu.SMEM)
    hbm = pl.BlockSpec(memory_space=pl.ANY)

    def exchange(value, who):
        return lax.all_to_all(value, AXES, split_axis=0, concat_axis=0, axis_index_groups=who, tiled=True)

    def swap(value):
        return lax.ppermute(value, "c", [(0, 1), (1, 0)])

    at = 16 * (2 * (lax.axis_index("z") % 2) + lax.axis_index("yl"))
    near = exchange(
        pl.pallas_call(
            scale_kernel,
            out_shape=jax.ShapeDtypeStruct((16, 16, 192), BF),
            in_specs=[smem, vmem, smem],
            out_specs=vmem,
            name="scale",
        )(at.reshape(1), codes, code_scale),
        near_groups,
    )
    own, send = pl.pallas_call(
        term_kernel,
        out_shape=[jax.ShapeDtypeStruct((8, HD, 768), BF)] * 2,
        in_specs=[smem, hbm, vmem],
        out_specs=[hbm, hbm],
        scratch_shapes=[
            pltpu.VMEM((8, TOK, 1536), BF),
            pltpu.VMEM((8 * HD, 768), BF),
            pltpu.VMEM((2, 8, HD, 768), BF),
            pltpu.SemaphoreType.DMA((8,)),
            pltpu.SemaphoreType.DMA((4,)),
        ],
        compiler_params=pltpu.CompilerParams(vmem_limit_bytes=60 * 2**20),
        cost_estimate=pl.CostEstimate(flops=2 * D * TOK * HD, bytes_accessed=5 * 2**20, transcendentals=0),
        name="term",
    )(core, tokens, upstream.T)
    send, near = lax.optimization_barrier((send, near))
    part = pl.BlockSpec((4, HD, 768), lambda i: (i, 0, 0))
    outgoing = pl.pallas_call(
        fill_kernel,
        grid=(2,),
        out_shape=jax.ShapeDtypeStruct((8, HD, 1536), BF),
        in_specs=[pl.BlockSpec((16, 16, 192), lambda i: (0, 0, 0)), part, part],
        out_specs=pl.BlockSpec((4, HD, 1536), lambda i: (i, 0, 0)),
        compiler_params=pltpu.CompilerParams(vmem_limit_bytes=40 * 2**20),
        name="fill",
    )(near, own, swap(send))
    arrived = exchange(outgoing, cube)
    partial_sum, *weights = pl.pallas_call(
        sum_kernel,
        grid=(2,),
        out_shape=[jax.ShapeDtypeStruct((64, 8, 128), BF)] + [jax.ShapeDtypeStruct((SHARE, HD, 768), BF)] * (8 // SHARE),
        in_specs=[pl.BlockSpec((8, HD, SPAN), lambda i: (0, 0, i)), hbm],
        out_specs=[pl.BlockSpec((32, 8, 128), lambda i: (i, 0, 0))] + [hbm] * (8 // SHARE),
        scratch_shapes=[pltpu.SemaphoreType.DMA((8 // SHARE,))],
        compiler_params=pltpu.CompilerParams(vmem_limit_bytes=40 * 2**20),
        cost_estimate=pl.CostEstimate(flops=2 * D * HD, bytes_accessed=2 * 2**20, transcendentals=0),
        name="sum",
    )(arrived, arrived)
    last = exchange(partial_sum, rest)
    values = pl.pallas_call(
        values_kernel,
        out_shape=jax.ShapeDtypeStruct((HD, TOK), BF),
        in_specs=[smem] + [vmem] * (16 // SHARE + 1),
        out_specs=vmem,
        compiler_params=pltpu.CompilerParams(vmem_limit_bytes=52 * 2**20),
        cost_estimate=pl.CostEstimate(flops=2 * D * TOK * HD, bytes_accessed=5 * 2**20, transcendentals=0),
        name="values",
    )(core, *weights, *[swap(piece) for piece in weights], tokens)
    last, values = lax.optimization_barrier((last, values))
    weight_grad = pl.pallas_call(
        final_kernel,
        out_shape=jax.ShapeDtypeStruct((12, HD), F32),
        in_specs=[vmem],
        out_specs=vmem,
        compiler_params=pltpu.CompilerParams(vmem_limit_bytes=4 * 2**20),
        name="final",
    )(last)
    return values.T, weight_grad


def solution(mesh):
    fine = Mesh(mesh.devices.reshape(SIZES), AXES)
    rows = P(AXES, None)
    columns = P(None, ("yh", "x", "c"))
    return jax.shard_map(
        shards, mesh=fine, in_specs=(rows, columns, columns, rows), out_specs=(rows, rows), check_vma=False
    )
```

```python
import jax
import jax.numpy as jnp
import numpy as np
from jax import lax
from jax.experimental import pallas as pl
from jax.experimental.pallas import tpu as pltpu
from jax.sharding import Mesh
from jax.sharding import PartitionSpec as P

AXES = ("z", "yl", "yh", "x", "c")
SIZES = (8, 2, 4, 8, 2)
D, HD, TOK = 12288, 64, 128
SHARE = 2
BF, F32 = jnp.bfloat16, jnp.float32
NT = (((1,), (1,)), ((), ()))
SPAN = 384


def groups():
    dev = np.arange(1024).reshape(SIZES)
    whole = dev.transpose(0, 2, 1, 3, 4).reshape(8, 8, 8, 2)
    near = [dev[z, yl, :, px::2, c].reshape(-1) for c in range(2) for z in range(8) for yl in range(2) for px in range(2)]
    rest = [dev[pz::2, yl, :, px::2, c].reshape(-1) for c in range(2) for pz in range(2) for yl in range(2) for px in range(2)]
    cube = []
    for core in range(2):
        for base in np.ndindex(4, 4, 4):
            corner = [2 * i + core for i in base]
            members = {}
            for step in np.ndindex(2, 2, 2):
                z, y, x = [(i + j) % 8 for i, j in zip(corner, step)]
                members[z % 2 * 4 + y % 2 * 2 + x % 2] = whole[z, y, x, core]
            cube.append(np.array([members[k] for k in range(8)]))
    return [[g.tolist() for g in kind] for kind in (near, cube, rest)]


def scale_kernel(at_ref, codes_ref, scale_ref, out_ref):
    lane = lax.broadcasted_iota(jnp.int32, (16, 192), 1) // 32
    factor = jnp.full((16, 192), scale_ref[0, 0], F32)
    for k in range(1, 6):
        factor = jnp.where(lane == k, scale_ref[0, k], factor)
    rows = codes_ref[pl.ds(pl.multiple_of(at_ref[0], 16), 16), :]
    weights = (rows.astype(F32) * factor).astype(BF)
    for k in range(16):
        out_ref[k] = weights


def term_kernel(core_ref, tokens_hbm, upstream_ref, own_hbm, send_hbm, tokens_ref, part_ref, out_ref, in_sem, out_sem):
    core = core_ref[0]
    reads = [
        pltpu.make_async_copy(tokens_hbm.at[:, 1536 * z : 1536 * (z + 1)], tokens_ref.at[z], in_sem.at[z])
        for z in range(8)
    ]
    for read in reads:
        read.start()
    source = lax.broadcasted_iota(jnp.int32, (768, 1), 0)
    place = lax.broadcasted_iota(jnp.int32, (768, 768), 1)
    line = source // 12
    target = 12 * (32 * (line % 2) + 16 * (line // 2 % 2) + line // 4) + source % 12
    move = (place == target).astype(F32).astype(BF)
    writes = []
    for half in range(2):
        for z in range(4):
            reads[4 * half + z].wait()
            part = jnp.dot(upstream_ref[...], tokens_ref[4 * half + z], preferred_element_type=F32).astype(BF)
            for yl in range(2):
                part_ref[HD * (2 * z + yl) : HD * (2 * z + yl + 1)] = part[:, 768 * yl : 768 * (yl + 1)]
        for owner in range(2):
            moved = jnp.dot(
                part_ref[...], move[:, SPAN * owner : SPAN * (owner + 1)], preferred_element_type=F32
            ).astype(BF)
            for z in range(4):
                for yl in range(2):
                    for px in range(2):
                        k = z % 2 * 4 + yl * 2 + px
                        at = SPAN * half + 192 * (z // 2)
                        out_ref[owner, k, :, at : at + 192] = moved[
                            HD * (2 * z + yl) : HD * (2 * z + yl + 1), 192 * px : 192 * (px + 1)
                        ]
        at = pl.ds(SPAN * half, SPAN)
        for i, (owner, out_hbm) in enumerate(((1 - core, send_hbm), (core, own_hbm))):
            writes.append(
                pltpu.make_async_copy(out_ref.at[owner, :, :, at], out_hbm.at[:, :, at], out_sem.at[2 * half + i])
            )
            writes[-1].start()
    for write in writes:
        write.wait()


def keep_kernel(in_hbm, out_ref, sem):
    copy = pltpu.make_async_copy(in_hbm, out_ref, sem)
    copy.start()
    copy.wait()


def fill_kernel(near_ref, own_ref, other_ref, out_ref):
    out_ref[:, :, :768] = (own_ref[...].astype(F32) + other_ref[...].astype(F32)).astype(BF)
    for p in range(out_ref.shape[0]):
        for k in range(16):
            out_ref[p, 16 * (k // 4) : 16 * (k // 4 + 1), 768 + 192 * (k % 4) : 960 + 192 * (k % 4)] = near_ref[k]


def sum_kernel(in_ref, in_hbm, out_ref, *refs):
    step = pl.program_id(0)
    weights, sem = refs[:-1], refs[-1]
    copies = [
        pltpu.make_async_copy(in_hbm.at[pl.ds(SHARE * i, SHARE), :, pl.ds(768, 768)], piece, sem.at[i])
        for i, piece in enumerate(weights)
    ]

    @pl.when(step == 0)
    def _():
        for copy in copies:
            copy.start()

    row = lax.broadcasted_iota(jnp.int32, (256, 1), 0)
    col = lax.broadcasted_iota(jnp.int32, (256, SPAN), 1)
    first = jnp.where(row % 8 < 6, 12 * (row // 8) + row % 8, -SPAN)
    pick = jnp.concatenate([(col == first).astype(F32), (col == first + 6).astype(F32)], axis=1).astype(BF)
    total = in_ref[0].astype(F32)
    for k in range(1, 8):
        total += in_ref[k].astype(F32)
    total = total.astype(BF)
    blank = jnp.zeros((HD, SPAN), BF)
    both = jnp.concatenate(
        [jnp.concatenate([total, blank], axis=1), jnp.concatenate([blank, total], axis=1)], axis=0
    )
    rows = lax.dot_general(pick, both, NT, preferred_element_type=F32)
    out_ref[...] = rows.reshape(32, 8, 128).astype(BF)

    @pl.when(step == 1)
    def _():
        for copy in copies:
            copy.wait()


def values_kernel(core_ref, *refs):
    tokens_ref, out_ref = refs[-2:]
    own, other = refs[: 8 // SHARE], refs[8 // SHARE : -2]

    def product(first, second):
        total = jnp.zeros((HD, TOK), F32)
        for yh in range(4):
            for x in range(8):
                at = SPAN * (yh * 8 + x)
                halves = [
                    jnp.concatenate(
                        [
                            pieces[(2 * q + x % 2) // SHARE][(2 * q + x % 2) % SHARE, 16 * yh : 16 * (yh + 1), 192 * (x // 2) : 192 * (x // 2 + 1)]
                            for q in range(4)
                        ],
                        axis=0,
                    )
                    for pieces in (first, second)
                ]
                total += lax.dot_general(
                    jnp.concatenate(halves, axis=1), tokens_ref[:, at : at + SPAN], NT, preferred_element_type=F32
                )
        out_ref[...] = total.astype(BF)

    @pl.when(core_ref[0] == 0)
    def _():
        product(own, other)

    @pl.when(core_ref[0] != 0)
    def _():
        product(other, own)


def final_kernel(in_ref, out_ref):
    total = in_ref[0].astype(F32)
    for k in range(1, 64):
        total += in_ref[k].astype(F32)
    out_ref[0:6] = total[0:6, :HD]
    out_ref[6:12] = total[0:6, HD:]


def shards(tokens, codes, code_scale, upstream):
    near_groups, cube, rest = groups()
    core = lax.axis_index("c").reshape(1)
    vmem = pl.BlockSpec(memory_space=pltpu.VMEM)
    smem = pl.BlockSpec(memory_space=pltpu.SMEM)
    hbm = pl.BlockSpec(memory_space=pl.ANY)

    def exchange(value, who):
        return lax.all_to_all(value, AXES, split_axis=0, concat_axis=0, axis_index_groups=who, tiled=True)

    def swap(value):
        return lax.ppermute(value, "c", [(0, 1), (1, 0)])

    at = 16 * (2 * (lax.axis_index("z") % 2) + lax.axis_index("yl"))
    near = exchange(
        pl.pallas_call(
            scale_kernel,
            out_shape=jax.ShapeDtypeStruct((16, 16, 192), BF),
            in_specs=[smem, vmem, smem],
            out_specs=vmem,
            name="scale",
        )(at.reshape(1), codes, code_scale),
        near_groups,
    )
    own, send = pl.pallas_call(
        term_kernel,
        out_shape=[jax.ShapeDtypeStruct((8, HD, 768), BF)] * 2,
        in_specs=[smem, hbm, vmem],
        out_specs=[hbm, hbm],
        scratch_shapes=[
            pltpu.VMEM((8, TOK, 1536), BF),
            pltpu.VMEM((8 * HD, 768), BF),
            pltpu.VMEM((2, 8, HD, 768), BF),
            pltpu.SemaphoreType.DMA((8,)),
            pltpu.SemaphoreType.DMA((4,)),
        ],
        compiler_params=pltpu.CompilerParams(vmem_limit_bytes=60 * 2**20),
        cost_estimate=pl.CostEstimate(flops=2 * D * TOK * HD, bytes_accessed=5 * 2**20, transcendentals=0),
        name="term",
    )(core, tokens, upstream.T)
    send, near = lax.optimization_barrier((send, near))
    own = pl.pallas_call(
        keep_kernel,
        out_shape=jax.ShapeDtypeStruct((8, HD, 768), BF),
        in_specs=[hbm],
        out_specs=vmem,
        scratch_shapes=[pltpu.SemaphoreType.DMA],
        compiler_params=pltpu.CompilerParams(vmem_limit_bytes=8 * 2**20),
        cost_estimate=pl.CostEstimate(flops=0, bytes_accessed=4 * 2**20, transcendentals=0),
        name="keep",
    )(own)
    part = pl.BlockSpec((4, HD, 768), lambda i: (i, 0, 0))
    outgoing = pl.pallas_call(
        fill_kernel,
        grid=(2,),
        out_shape=jax.ShapeDtypeStruct((8, HD, 1536), BF),
        in_specs=[pl.BlockSpec((16, 16, 192), lambda i: (0, 0, 0)), part, part],
        out_specs=pl.BlockSpec((4, HD, 1536), lambda i: (i, 0, 0)),
        compiler_params=pltpu.CompilerParams(vmem_limit_bytes=40 * 2**20),
        name="fill",
    )(near, own, swap(send))
    arrived = exchange(outgoing, cube)
    partial_sum, *weights = pl.pallas_call(
        sum_kernel,
        grid=(2,),
        out_shape=[jax.ShapeDtypeStruct((64, 8, 128), BF)] + [jax.ShapeDtypeStruct((SHARE, HD, 768), BF)] * (8 // SHARE),
        in_specs=[pl.BlockSpec((8, HD, SPAN), lambda i: (0, 0, i)), hbm],
        out_specs=[pl.BlockSpec((32, 8, 128), lambda i: (i, 0, 0))] + [hbm] * (8 // SHARE),
        scratch_shapes=[pltpu.SemaphoreType.DMA((8 // SHARE,))],
        compiler_params=pltpu.CompilerParams(vmem_limit_bytes=40 * 2**20),
        cost_estimate=pl.CostEstimate(flops=2 * D * HD, bytes_accessed=2 * 2**20, transcendentals=0),
        name="sum",
    )(arrived, arrived)
    last = exchange(partial_sum, rest)
    values = pl.pallas_call(
        values_kernel,
        out_shape=jax.ShapeDtypeStruct((HD, TOK), BF),
        in_specs=[smem] + [vmem] * (16 // SHARE + 1),
        out_specs=vmem,
        compiler_params=pltpu.CompilerParams(vmem_limit_bytes=52 * 2**20),
        cost_estimate=pl.CostEstimate(flops=2 * D * TOK * HD, bytes_accessed=5 * 2**20, transcendentals=0),
        name="values",
    )(core, *weights, *[swap(piece) for piece in weights], tokens)
    last, values = lax.optimization_barrier((last, values))
    weight_grad = pl.pallas_call(
        final_kernel,
        out_shape=jax.ShapeDtypeStruct((12, HD), F32),
        in_specs=[vmem],
        out_specs=vmem,
        compiler_params=pltpu.CompilerParams(vmem_limit_bytes=4 * 2**20),
        name="final",
    )(last)
    return values.T, weight_grad


def solution(mesh):
    fine = Mesh(mesh.devices.reshape(SIZES), AXES)
    rows = P(AXES, None)
    columns = P(None, ("yh", "x", "c"))
    return jax.shard_map(
        shards, mesh=fine, in_specs=(rows, columns, columns, rows), out_specs=(rows, rows), check_vma=False
    )
```
